128 devices in a mesh: path: 32 (over y, z, x_lo), section: 4 (over x_hi, core).
Axes of the slice: x: 4 (x_hi: 2, x_lo: 2; x = x_hi * 2 + x_lo), y: 4, z: 4, core: 2. Of those that a mesh axis runs over, the one named last changes fastest.
Arguments:
- delta: bfloat16 [4, 32, 2048, 1024], P('section', 'path'), may hold values from -0.1796875 to 0.1796875
- outer_params: float32 [4, 16, 2048, 1024], P('section', None, 'path'), may hold values from -0.125 to 0.125
- momentum: float32 [4, 16, 2048, 1024], P('section', None, 'path'), may hold values from -0.06 to 0.06
- module_table: int32 [4, 32, 1], P('section'), may hold values from 0 to 15
- token_ids: int32 [32, 512], P('path'), may hold values from 0 to 15999
- embedding: bfloat16 [16000, 2048], P(None, 'path'), may hold values from -6 to 6
Outputs:
- new_params: float32 [4, 16, 2048, 1024], P('section', None, 'path')
- new_momentum: float32 [4, 16, 2048, 1024], P('section', None, 'path')
- level_outputs: bfloat16 [4, 32, 512, 2048], P('section', 'path')
The draws below stay inside these ranges and needn't reach their ends.
Inputs may be any that keep to these rules, and one draw needn't show every extreme that they name: `module_table`: each value of 0 to 15 appears somewhere in the table.
All inputs are finite; a program needn't handle non-finite values.
Results may differ from the reference program's by a relative error of at most 0.0059.
Values may be sent and summed in bfloat16 or wider, within the bound.
A program may use at most 128 MiB of HBM per device.

```python
import math
import jax
import jax.numpy as jnp
import numpy as np
from jax import lax

D = 2048
DW = 1024
MODULES = 16
VOCAB = 16000
TOK = 512
LEVELS = 4
PATHS = 32


def plant(array, key, low, top_value):
    extent = array.shape
    spot = [jax.random.randint(jax.random.fold_in(key, axis), (), 0, extent[axis]) for axis in range(len(extent))]
    array = array.at[tuple(spot)].set(low)
    longest = extent.index(max(extent))
    spot[longest] = (spot[longest] + 1) % extent[longest]
    return array.at[tuple(spot)].set(top_value)


def block_scale(rng, shape, pieces, smallest, largest):
    def one(axis_at, blocks):
        heights = jax.random.uniform(jax.random.fold_in(jax.random.fold_in(rng, 6), axis_at), (blocks,), jnp.float32, smallest / len(pieces), largest / len(pieces))
        return jnp.repeat(jnp.exp(heights), shape[axis_at] // blocks).reshape((-1,) + (1,) * (len(shape) - axis_at - 1))

    factor_of = one(*pieces[0])
    for cut in pieces[1:]:
        factor_of = factor_of * one(*cut)
    return factor_of


def rank_table(count, slope):
    loads = [(1 << 20) // math.isqrt(rank ** slope) + 1 for rank in range(1, count + 1)]
    spread = 1 + sum(loads) // (1 << 30)
    return np.cumsum(np.array([max(1, weight // spread) for weight in loads]))


def ranked_ids(own_key, dims, count, skew):
    listing = rank_table(count, skew)
    pick = jax.random.randint(jax.random.fold_in(own_key, 1), dims, 0, int(listing[count - 1]))
    rank = jnp.searchsorted(jnp.asarray(listing, jnp.int32), pick, side="right")
    return jax.random.permutation(jax.random.fold_in(own_key, 2), count)[rank].astype(jnp.int32)


def picks_of(key, rows, number_of, top, lift):
    ranking = jax.random.permutation(jax.random.fold_in(key, 1), number_of)
    favour = ranking
    for power in range(3):
        favour = favour * favour // number_of
    favour = favour * lift // number_of
    lots = jax.random.randint(jax.random.fold_in(key, 2), (rows, number_of), 0, 4096) + favour
    sure = jax.random.permutation(jax.random.fold_in(key, 3), rows)[jnp.arange(number_of) % rows]
    lots = jnp.where(jnp.arange(rows)[:, None] == sure[None, :], 1 << 14, lots)
    score = lots * number_of + jnp.arange(number_of)
    return lax.top_k(score.astype(jnp.int32), top)[1].astype(jnp.int32)


def normal_values(own_key, shape, width, most, cuts=(), kind=jnp.bfloat16):
    factor_of = block_scale(own_key, shape, cuts, -0.22, 0.18) if cuts else 1.0
    array = jax.random.normal(own_key, shape, jnp.float32) * width * factor_of
    return jnp.minimum(jnp.maximum(array, -most), most).astype(kind)


def setup_inputs(seed: int = 0) -> dict:
    key_of = jax.random.split(jax.random.key(seed), 7)
    delta = normal_values(key_of[0], (LEVELS, PATHS, D, DW), 0.03, 0.1796875, ((0, 4), (1, 32)))
    outer_params = normal_values(key_of[1], (LEVELS, MODULES, D, DW), D ** -0.5, 0.125, ((0, 4), (2, 32)), jnp.float32)
    momentum = normal_values(key_of[2], (LEVELS, MODULES, D, DW), 0.01, 0.06, ((0, 4), (2, 32)), jnp.float32)
    module_table = picks_of(key_of[3], LEVELS * PATHS, MODULES, 1, 1024).reshape((LEVELS, PATHS, 1))
    token_ids = plant(ranked_ids(key_of[4], (PATHS, TOK), VOCAB, 2), jax.random.fold_in(key_of[4], 3), 0, VOCAB - 1).astype(jnp.int32)
    embedding = normal_values(key_of[5], (VOCAB, D), 1.0, 6.0, ((1, 32),))
    return dict(delta=delta, outer_params=outer_params, momentum=momentum, module_table=module_table, token_ids=token_ids, embedding=embedding)


def apply_level(acts, weights):
    values = acts.astype(jnp.float32)
    scale = lax.rsqrt(lax.optimization_barrier(jnp.mean(values * values, axis=-1, keepdims=True)) + 1e-06)
    normed = (values * scale).astype(jnp.bfloat16)
    mixed = jnp.einsum('ptd,pdc->ptc', normed.astype(jnp.float32), weights.astype(jnp.float32))
    written = values[..., :DW] + jax.nn.silu(mixed)
    return jnp.concatenate([written, values[..., DW:]], axis=-1).astype(jnp.bfloat16)

def reference(delta, outer_params, momentum, module_table, token_ids, embedding):
    params_list = []
    moment_list = []
    weight_list = []
    for level in range(LEVELS):
        chosen = module_table[level, :, 0].astype(jnp.int32)
        sums = jax.ops.segment_sum(delta[level].astype(jnp.float32), chosen, num_segments=MODULES)
        counts = jax.ops.segment_sum(jnp.ones((PATHS,), jnp.float32), chosen, num_segments=MODULES)
        grad = sums / jnp.maximum(counts, 1.0)[:, None, None]
        moment_next = 0.9 * momentum[level] + grad
        params_next = outer_params[level] - 0.7 * (grad + 0.9 * moment_next)
        params_list.append(params_next)
        moment_list.append(moment_next)
        weight_list.append(jnp.take(params_next.astype(jnp.bfloat16), chosen, axis=0))
    acts = jnp.take(embedding, token_ids.reshape(-1), axis=0).reshape(PATHS, TOK, D)
    outputs = []
    for level in range(LEVELS):
        acts = apply_level(acts, weight_list[level])
        outputs.append(acts)
    return (jnp.stack(params_list), jnp.stack(moment_list), jnp.stack(outputs))
```

```python
import functools

import jax
import jax.numpy as jnp
from jax import lax
from jax.experimental import pallas as pl
from jax.experimental.pallas import tpu as pltpu
from jax.sharding import PartitionSpec as P

MESH = pl.DeviceIdType.MESH
STEPS = [(y, z, x) for y in range(4) for z in range(4) for x in range(2)][1:]
ORDER = sorted(STEPS, key=lambda t: ((t[0] * 5 + t[1] * 3 + t[2] * 7) % 11, t))


def shifted(me, step):
    y, z, x = step
    return (
        lax.rem(me // 8 + y, 4) * 8
        + lax.rem(lax.rem(me // 2, 4) + z, 4) * 2
        + lax.rem(lax.rem(me, 2) + x, 2)
    )


def kernel(
    delta, params, moment, table_t, ids, chosen,
    out_params, out_moment, out_acts,
    pieces, par, mom, fresh, sending, weight,
    columns, table, id_own, id_all, id_scalar, gathered, leaving, arrived,
    x_first, x_rest, o_first, partial,
    local_sem, id_sem, delta_send, delta_recv, weight_send, weight_recv,
    lookup_send, lookup_recv, core_sem, level_send, level_recv,
):
    me = lax.axis_index("path")
    sec = lax.axis_index("section")
    half = lax.rem(sec, 2)
    mate = sec + 1 - 2 * half
    paths, rows = pieces.shape[0], pieces.shape[1]
    modules = par.shape[0]
    wide = par.shape[2]
    width = table.shape[1]
    others = paths - 1
    late = sec >= 2

    def remote(src, dst, send, recv, path, section):
        return pltpu.make_async_remote_copy(
            src_ref=src, dst_ref=dst, send_sem=send, recv_sem=recv,
            device_id=(path, section), device_id_type=MESH,
        )

    loads = [
        pltpu.make_async_copy(table_t, columns, local_sem.at[0]),
        pltpu.make_async_copy(params, par, local_sem.at[1]),
        pltpu.make_async_copy(moment, mom, local_sem.at[2]),
    ]
    for load in loads:
        load.start()
    tiles = ids.shape[1] // 128
    for tile in range(tiles):
        id_own[tile:tile + 1, :] = ids[:, 128 * tile:128 * (tile + 1)]
    id_own[tiles:, :] = jnp.zeros((8 - tiles, 128), jnp.int32)
    id_all[me] = id_own[...]

    barrier = pltpu.get_barrier_semaphore()
    for step in ORDER:
        pl.semaphore_signal(barrier, inc=1, device_id=(shifted(me, step), sec), device_id_type=MESH)

    @pl.when(sec > 0)
    def _():
        pl.semaphore_signal(barrier, inc=1, device_id=(me, sec - 1), device_id_type=MESH)

    @pl.when(sec < 3)
    def _():
        pl.semaphore_signal(barrier, inc=1, device_id=(me, sec + 1), device_id_type=MESH)

    pl.semaphore_wait(barrier, others + jnp.where(sec > 0, 1, 0) + jnp.where(sec < 3, 1, 0))

    for step in ORDER:
        to = shifted(me, step)
        remote(id_own, id_all.at[me], id_sem.at[0], id_sem.at[1], to, sec).start()
    part = rows // 2
    for piece in range(2):
        span = pl.ds(piece * part, part)
        for step in ORDER:
            to = shifted(me, step)
            remote(
                delta.at[to, span], pieces.at[me, span],
                delta_send.at[piece], delta_recv.at[piece], to, sec,
            ).start()
        pltpu.make_async_copy(delta.at[me, span], pieces.at[me, span], local_sem.at[3 + piece]).start()

    loads[0].wait()

    @pl.loop(0, table.shape[0] // 128)
    def _(block):
        start = pl.multiple_of(block * 128, 128)
        table[pl.ds(start, 128), :] = columns[:, pl.ds(start, 128)].astype(jnp.float32).T

    everyone = id_all.at[pl.ds(0, others)]
    remote(everyone, everyone, id_sem.at[0], id_sem.at[1], me, sec).wait_recv()
    ids_in = pltpu.make_async_copy(id_all, id_scalar, local_sem.at[5])
    ids_in.start()
    ids_in.wait()

    tokens = gathered.shape[0]
    holds = jnp.logical_or(sec < 2, me >= paths // 2)
    own_rows = pl.ds(pl.multiple_of(me * width, width), width)

    @pl.when(holds)
    def _():
        @pl.loop(0, paths)
        def _(turn):
            to = shifted(me, (turn // 8, lax.rem(turn // 2, 4), lax.rem(turn, 2)))

            @pl.loop(0, tokens // 16)
            def _(group):
                line = half * (tokens // 128) + group // 8
                first = lax.rem(group, 8) * 16
                for at in range(16):
                    token = id_scalar[to, line, first + at]
                    gathered[pl.ds(group * 16 + at, 1), :] = table[pl.ds(token, 1), :]

            leaving[to] = gathered[...].T.astype(jnp.bfloat16)

            @pl.when(turn > 0)
            def _():
                remote(
                    leaving.at[to], arrived.at[half, own_rows],
                    lookup_send, lookup_recv, to, sec,
                ).start()

        arrived[half, own_rows, :] = leaving[me]

    loads[1].wait()
    loads[2].wait()
    group_rows = 16
    pair_rows, pair_cols = modules * group_rows, paths * group_rows
    col = lax.broadcasted_iota(jnp.int32, (1, pair_cols), 1)
    uses = jnp.zeros((1, pair_cols), jnp.int32)
    for path in range(paths):
        uses = jnp.where(col // group_rows == path, chosen[path], uses)
    row = lax.broadcasted_iota(jnp.int32, (pair_rows, pair_cols), 0)
    cols = lax.broadcasted_iota(jnp.int32, (pair_rows, pair_cols), 1)
    match = (uses == row // group_rows) & (lax.rem(row, group_rows) == lax.rem(cols, group_rows))
    match = match.astype(jnp.float32)
    counts = jnp.maximum(jnp.sum(match, axis=1, keepdims=True), 1.0)
    match = match.astype(jnp.bfloat16)
    lanes = 256
    for piece in range(2):
        span = pl.ds(piece * part, part)
        landed = pieces.at[pl.ds(0, others), span]
        remote(landed, landed, delta_send.at[piece], delta_recv.at[piece], me, sec).wait_recv()
        pltpu.make_async_copy(delta.at[me, span], pieces.at[me, span], local_sem.at[3 + piece]).wait()
        for group in range(part // group_rows):
            at = pl.ds(piece * part + group * group_rows, group_rows)

            @pl.loop(0, wide // lanes)
            def _(block):
                cut = pl.ds(pl.multiple_of(block * lanes, lanes), lanes)
                terms = pieces[:, at, cut].reshape(pair_cols, lanes)
                sums = jnp.dot(match, terms, preferred_element_type=jnp.float32)
                grad = sums / counts
                moved = 0.9 * mom[:, at, cut].reshape(pair_rows, lanes) + grad
                stepped = par[:, at, cut].reshape(pair_rows, lanes) - 0.7 * (grad + 0.9 * moved)
                mom[:, at, cut] = moved.reshape(modules, group_rows, lanes)
                par[:, at, cut] = stepped.reshape(modules, group_rows, lanes)
                fresh[:, at, cut] = stepped.astype(jnp.bfloat16).reshape(modules, group_rows, lanes)

        pltpu.make_async_copy(par.at[:, span], out_params.at[:, span], local_sem.at[6 + piece]).start()
        pltpu.make_async_copy(mom.at[:, span], out_moment.at[:, span], local_sem.at[8 + piece]).start()

        @pl.loop(0, paths)
        def _(path):
            sending[path, span, :] = fresh[chosen[path], span, :]

        weight[me, span, :] = sending[me, span, :]
        for step in ORDER:
            to = shifted(me, step)
            remote(
                sending.at[to, span], weight.at[me, span],
                weight_send.at[piece], weight_recv.at[piece], to, sec,
            ).start()

    def lookups(count):
        span = arrived.at[half, pl.ds(0, count * width)]
        return remote(span, span, lookup_send, lookup_recv, me, sec)

    @pl.when(sec < 2)
    def _():
        lookups(others).wait_recv()

    @pl.when(jnp.logical_and(late, me >= paths // 2))
    def _():
        lookups(paths // 2 - 1).wait_recv()

    @pl.when(jnp.logical_and(late, me < paths // 2))
    def _():
        lookups(paths // 2).wait_recv()

    model = arrived.shape[1]
    mid = model // 2
    upper = arrived.at[half, pl.ds(mid, mid)]
    lower = arrived.at[half, pl.ds(0, mid)]
    upper_copy = remote(upper, upper, core_sem.at[0], core_sem.at[1], me, mate)
    lower_copy = remote(lower, lower, core_sem.at[2], core_sem.at[3], me, mate)
    upper_copy.start()

    @pl.when(sec == 1)
    def _():
        lower_copy.start()

    other_upper = arrived.at[1 - half, pl.ds(mid, mid)]
    other_lower = arrived.at[1 - half, pl.ds(0, mid)]
    remote(other_upper, other_upper, core_sem.at[0], core_sem.at[1], me, mate).wait_recv()

    def turned(dst, first):
        for side in range(2):
            @pl.loop(0, mid // 256)
            def _(block):
                start = pl.multiple_of(block * 256, 256)
                tile = arrived[side, pl.ds(first + start, 256), :].astype(jnp.float32)
                dst[pl.ds(side * tokens, tokens), pl.ds(start, 256)] = tile.T.astype(jnp.bfloat16)

    turned(x_rest, mid)

    @pl.when(sec == 0)
    def _():
        remote(other_lower, other_lower, core_sem.at[2], core_sem.at[3], me, mate).wait_recv()
        turned(x_first, 0)

    rest_out = pltpu.make_async_copy(x_rest, out_acts.at[:, pl.ds(mid, mid)], local_sem.at[10])
    rest_out.start()

    for piece in range(2):
        span = pl.ds(piece * part, part)
        landed = weight.at[pl.ds(0, others), span]
        remote(landed, landed, weight_send.at[piece], weight_recv.at[piece], me, sec).wait_recv()

    blocks = level_send.shape[0]
    size = x_first.shape[0] // blocks
    for block in range(blocks):
        at = pl.ds(block * size, size)

        @pl.loop(0, wide // lanes)
        def _(cut_at):
            cut = pl.ds(pl.multiple_of(cut_at * lanes, lanes), lanes)
            partial[at, cut] = jnp.dot(
                x_rest[at, :], weight[paths // 2:, :, cut].reshape(mid, lanes),
                preferred_element_type=jnp.float32,
            )

    for block in range(blocks):
        at = pl.ds(block * size, size)
        here, there = x_first.at[at], o_first.at[at]
        hop = remote(there, here, level_send.at[block], level_recv.at[block], me, jnp.minimum(sec + 1, 3))

        @pl.when(sec > 0)
        def _():
            hop.wait_recv()

        firsts = x_first[at, :].astype(jnp.float32)
        rests = x_rest[at, :].astype(jnp.float32)
        squares = jnp.sum(firsts * firsts, axis=-1, keepdims=True) + jnp.sum(rests * rests, axis=-1, keepdims=True)
        scale = lax.rsqrt(squares / model + 1e-06)

        @pl.loop(0, wide // lanes)
        def _(cut_at):
            cut = pl.ds(pl.multiple_of(cut_at * lanes, lanes), lanes)
            mixed = scale * (partial[at, cut] + jnp.dot(
                x_first[at, :], weight[:paths // 2, :, cut].reshape(mid, lanes),
                preferred_element_type=jnp.float32,
            ))
            written = x_first[at, cut].astype(jnp.float32) + jax.nn.silu(mixed)
            o_first[at, cut] = written.astype(jnp.bfloat16)

        @pl.when(sec < 3)
        def _():
            hop.start()

        pltpu.make_async_copy(there, out_acts.at[at, pl.ds(0, mid)], local_sem.at[11 + block]).start()

    for block in range(blocks):
        at = pl.ds(block * size, size)
        here, there = x_first.at[at], o_first.at[at]
        hop = remote(there, here, level_send.at[block], level_recv.at[block], me, jnp.minimum(sec + 1, 3))

        @pl.when(sec < 3)
        def _():
            hop.wait_send()

        pltpu.make_async_copy(there, out_acts.at[at, pl.ds(0, mid)], local_sem.at[11 + block]).wait()
    rest_out.wait()
    remote(everyone, everyone, id_sem.at[0], id_sem.at[1], me, sec).wait_send()
    upper_copy.wait_send()

    @pl.when(sec == 1)
    def _():
        lower_copy.wait_send()

    @pl.when(holds)
    def _():
        span = leaving.at[pl.ds(0, others)]
        remote(span, span, lookup_send, lookup_recv, me, sec).wait_send()

    for piece in range(2):
        span = pl.ds(piece * part, part)
        landed = pieces.at[pl.ds(0, others), span]
        remote(landed, landed, delta_send.at[piece], delta_recv.at[piece], me, sec).wait_send()
        landed = weight.at[pl.ds(0, others), span]
        remote(landed, landed, weight_send.at[piece], weight_recv.at[piece], me, sec).wait_send()
        pltpu.make_async_copy(par.at[:, span], out_params.at[:, span], local_sem.at[6 + piece]).wait()
        pltpu.make_async_copy(mom.at[:, span], out_moment.at[:, span], local_sem.at[8 + piece]).wait()


def local(delta, outer_params, momentum, module_table, token_ids, embedding):
    paths = module_table.shape[1]
    _, modules, rows, wide = outer_params.shape
    vocab, width = embedding.shape
    tok = token_ids.shape[1]
    model = delta.shape[2]
    mid = model // 2
    blocks = 4
    bf16, f32 = jnp.bfloat16, jnp.float32
    anywhere = pl.BlockSpec(memory_space=pl.ANY)
    dma = pltpu.SemaphoreType.DMA
    new_params, new_moment, acts = pl.pallas_call(
        kernel,
        out_shape=(
            jax.ShapeDtypeStruct((modules, rows, wide), f32),
            jax.ShapeDtypeStruct((modules, rows, wide), f32),
            jax.ShapeDtypeStruct((tok, model), bf16),
        ),
        in_specs=[
            anywhere, anywhere, anywhere, anywhere,
            pl.BlockSpec(memory_space=pltpu.VMEM),
            pl.BlockSpec(memory_space=pltpu.SMEM),
        ],
        out_specs=(anywhere, anywhere, anywhere),
        scratch_shapes=[
            pltpu.VMEM((paths, rows, wide), bf16),
            pltpu.VMEM((modules, rows, wide), f32),
            pltpu.VMEM((modules, rows, wide), f32),
            pltpu.VMEM((modules, rows, wide), bf16),
            pltpu.VMEM((paths, rows, wide), bf16),
            pltpu.VMEM((paths, rows, wide), bf16),
            pltpu.VMEM((width, vocab), bf16),
            pltpu.VMEM((vocab, width), f32),
            pltpu.VMEM((8, 128), jnp.int32),
            pltpu.VMEM((paths, 8, 128), jnp.int32),
            pltpu.SMEM((paths, 8, 128), jnp.int32),
            pltpu.VMEM((tok // 2, width), f32),
            pltpu.VMEM((paths, width, tok // 2), bf16),
            pltpu.VMEM((2, model, tok // 2), bf16),
            pltpu.VMEM((tok, mid), bf16),
            pltpu.VMEM((tok, mid), bf16),
            pltpu.VMEM((tok, mid), bf16),
            pltpu.VMEM((tok, wide), f32),
            dma((16,)), dma((2,)), dma((2,)), dma((2,)), dma((2,)), dma((2,)),
            dma, dma, dma((4,)), dma((blocks,)), dma((blocks,)),
        ],
        compiler_params=pltpu.CompilerParams(
            collective_id=0, has_side_effects=True, vmem_limit_bytes=60 * 1024 * 1024,
        ),
        name="outer_step",
    )(
        delta.reshape(paths, rows, wide), outer_params[0], momentum[0],
        embedding.T, token_ids, module_table[0, :, 0],
    )
    return (new_params[None], new_moment[None], acts[None, None])


def solution(mesh):
    return jax.shard_map(
        local,
        mesh=mesh,
        in_specs=(
            P("section", "path", None, None),
            P("section", None, "path", None),
            P("section", None, "path", None),
            P("section", None, None),
            P("path", None),
            P(None, "path"),
        ),
        out_specs=(
            P("section", None, "path", None),
            P("section", None, "path", None),
            P("section", "path", None, None),
        ),
        check_vma=False,
    )
```

```python
import jax
import jax.numpy as jnp
from jax import lax
from jax.experimental import pallas as pl
from jax.experimental.pallas import tpu as pltpu
from jax.sharding import PartitionSpec as P

MESH = pl.DeviceIdType.MESH
ORDER = [
    (2, 2, 1), (0, 1, 0), (3, 2, 1), (0, 3, 0), (1, 2, 1), (1, 0, 0), (2, 3, 1), (3, 0, 0),
    (2, 1, 1), (0, 0, 1), (2, 2, 0), (1, 1, 0), (2, 1, 0), (3, 3, 0), (2, 3, 0), (1, 3, 0),
    (1, 2, 0), (0, 3, 1), (3, 2, 0), (3, 1, 0), (1, 1, 1), (0, 1, 1), (3, 3, 1), (2, 0, 0),
    (3, 1, 1), (3, 0, 1), (1, 3, 1), (0, 2, 0), (2, 0, 1), (1, 0, 1), (0, 2, 1),
]
PIECES = 4
GROUP = 16


def shifted(me, step):
    y, z, x = step
    return (
        lax.rem(me // 8 + y, 4) * 8
        + lax.rem(lax.rem(me // 2, 4) + z, 4) * 2
        + lax.rem(lax.rem(me, 2) + x, 2)
    )


def kernel(
    delta, params, moment, table_t, ids, chosen,
    par, mom, acts,
    pieces, fresh, sending, weight,
    columns, table, id_own, id_all, id_scalar, gathered, leaving, lower, upper,
    x_first, total, squares,
    local_sem, id_sem, delta_send, delta_recv, weight_send, weight_recv,
    lower_send, lower_recv, upper_send, upper_recv, forward_send, forward_recv,
    core_sem, level_send, level_recv,
):
    me = lax.axis_index("path")
    sec = lax.axis_index("section")
    half = lax.rem(sec, 2)
    mate = sec + 1 - 2 * half
    paths, rows, wide = pieces.shape
    modules = par.shape[0]
    width = table.shape[1]
    model = acts.shape[1]
    mid = model // 2
    cut_of = wide // PIECES
    others = paths - 1
    late = sec >= 2
    looks = half == 1
    holds_upper = me >= paths // 2
    reads = jnp.logical_or(late, holds_upper)
    twin = me + 1 - 2 * lax.rem(me, 2)

    def remote(src, dst, send, recv, path, section):
        return pltpu.make_async_remote_copy(
            src_ref=src, dst_ref=dst, send_sem=send, recv_sem=recv,
            device_id=(path, section), device_id_type=MESH,
        )

    def same(ref, send, recv):
        return remote(ref, ref, send, recv, me, sec)

    loads = [
        pltpu.make_async_copy(table_t, columns, local_sem.at[0]),
        pltpu.make_async_copy(params, par, local_sem.at[1]),
        pltpu.make_async_copy(moment, mom, local_sem.at[2]),
    ]
    for load in loads:
        load.start()
    cuts = [pl.ds(piece * cut_of, cut_of) for piece in range(PIECES)]
    own = [
        pltpu.make_async_copy(delta.at[me, :, cuts[piece]], pieces.at[me, :, cuts[piece]], local_sem.at[3 + piece])
        for piece in range(PIECES)
    ]
    for copy in own:
        copy.start()
    tiles = ids.shape[1] // 128
    for tile in range(tiles):
        id_own[tile:tile + 1, :] = ids[:, 128 * tile:128 * (tile + 1)]
    id_own[tiles:, :] = jnp.zeros((8 - tiles, 128), jnp.int32)
    id_all[me] = id_own[...]

    barrier = pltpu.get_barrier_semaphore()
    for step in ORDER:
        pl.semaphore_signal(barrier, inc=1, device_id=(shifted(me, step), sec), device_id_type=MESH)

    @pl.when(sec > 0)
    def _():
        pl.semaphore_signal(barrier, inc=1, device_id=(me, sec - 1), device_id_type=MESH)

    @pl.when(sec < 3)
    def _():
        pl.semaphore_signal(barrier, inc=1, device_id=(me, sec + 1), device_id_type=MESH)

    @pl.when(jnp.logical_or(sec == 0, sec == 3))
    def _():
        pl.semaphore_signal(barrier, inc=1, device_id=(twin, 3 - sec), device_id_type=MESH)

    pl.semaphore_wait(barrier, others + 2)

    @pl.when(looks)
    def _():
        for step in ORDER:
            remote(id_own, id_all.at[me], id_sem.at[0], id_sem.at[1], shifted(me, step), sec).start()

    def send_delta(piece):
        for step in ORDER:
            to = shifted(me, step)
            remote(
                delta.at[to, :, cuts[piece]], pieces.at[me, :, cuts[piece]],
                delta_send.at[piece], delta_recv.at[piece], to, sec,
            ).start()

    ahead = PIECES // 2
    for piece in range(ahead):
        send_delta(piece)

    tokens = gathered.shape[0]
    half_paths = paths // 2
    slot = lax.rem(me, half_paths)
    own_rows = pl.ds(pl.multiple_of(slot * width, width), width)
    everyone = id_all.at[pl.ds(0, others)]
    quarters = 4
    holders = half_paths // quarters
    spans = [pl.ds(at * holders * width, holders * width) for at in range(quarters)]

    @pl.when(looks)
    def _():
        loads[0].wait()

        @pl.loop(0, table.shape[0] // 640)
        def _(block):
            start = pl.multiple_of(block * 640, 640)
            table[pl.ds(start, 640), :] = columns[:, pl.ds(start, 640)].T.astype(jnp.float32)

        same(everyone, id_sem.at[0], id_sem.at[1]).wait_recv()
        ids_in = pltpu.make_async_copy(id_all, id_scalar, local_sem.at[0])
        ids_in.start()
        ids_in.wait()

        @pl.when(reads)
        def _():
            @pl.loop(0, paths)
            def _(turn):
                to = shifted(me, (turn // 8, lax.rem(turn // 2, 4), lax.rem(turn, 2)))
                to_twin = to + 1 - 2 * lax.rem(to, 2)

                @pl.loop(0, tokens // 16)
                def _(group):
                    line = group // 8
                    first = lax.rem(group, 8) * 16
                    for at in range(16):
                        token = id_scalar[to, line, first + at]
                        gathered[pl.ds(group * 16 + at, 1), :] = table[pl.ds(token, 1), :]

                leaving[to] = gathered[...].T.astype(jnp.bfloat16)

                @pl.when(jnp.logical_and(to_twin != me, jnp.logical_not(holds_upper)))
                def _():
                    remote(
                        leaving.at[to], lower.at[own_rows],
                        lower_send, lower_recv.at[slot // holders], to_twin, sec,
                    ).start()

                @pl.when(jnp.logical_and(to != me, holds_upper))
                def _():
                    remote(leaving.at[to], upper.at[own_rows], upper_send, upper_recv, to, sec).start()

        @pl.when(holds_upper)
        def _():
            upper[own_rows, :] = leaving[me]

        @pl.when(jnp.logical_and(sec == 3, jnp.logical_not(holds_upper)))
        def _():
            lower[own_rows, :] = leaving[twin]

    for piece in range(ahead, PIECES):
        send_delta(piece)

    upper_copy = remote(upper, upper, core_sem.at[0], core_sem.at[1], me, mate)

    def passing(at):
        return remote(
            lower.at[spans[at]], lower.at[spans[at]], forward_send.at[at], forward_recv.at[at], twin, sec - 3
        )

    def forward():
        @pl.when(sec == 3)
        def _():
            for at in range(quarters):
                mine = jnp.logical_and(slot // holders == at, jnp.logical_not(holds_upper))

                @pl.when(mine)
                def _():
                    same(lower.at[pl.ds(0, (holders - 1) * width)], lower_send, lower_recv.at[at]).wait_recv()

                @pl.when(jnp.logical_not(mine))
                def _():
                    same(lower.at[pl.ds(0, holders * width)], lower_send, lower_recv.at[at]).wait_recv()

                passing(at).start()

        @pl.when(holds_upper)
        def _():
            same(upper.at[pl.ds(0, mid - width)], upper_send, upper_recv).wait_recv()

        @pl.when(jnp.logical_not(holds_upper))
        def _():
            same(upper, upper_send, upper_recv).wait_recv()

        upper_copy.start()

    loads[1].wait()
    loads[2].wait()
    pair_rows, pair_cols = modules * GROUP, paths * GROUP
    col = lax.broadcasted_iota(jnp.int32, (1, pair_cols), 1)
    uses = jnp.zeros((1, pair_cols), jnp.int32)
    for path in range(paths):
        uses = jnp.where(col // GROUP == path, chosen[path], uses)
    row = lax.broadcasted_iota(jnp.int32, (pair_rows, pair_cols), 0)
    cols = lax.broadcasted_iota(jnp.int32, (pair_rows, pair_cols), 1)
    match = (uses == row // GROUP) & (lax.rem(row, GROUP) == lax.rem(cols, GROUP))
    match = match.astype(jnp.float32)
    counts = jnp.maximum(jnp.sum(match, axis=1, keepdims=True), 1.0)
    match = match.astype(jnp.bfloat16)
    for piece in range(PIECES):
        if piece == ahead:
            pl.when(looks)(forward)
        cut = cuts[piece]
        same(pieces.at[pl.ds(0, others), :, cut], delta_send.at[piece], delta_recv.at[piece]).wait_recv()
        own[piece].wait()

        @pl.loop(0, rows // GROUP)
        def _(group):
            at = pl.ds(pl.multiple_of(group * GROUP, GROUP), GROUP)
            terms = pieces[:, at, cut].reshape(pair_cols, cut_of)
            sums = jnp.dot(match, terms, preferred_element_type=jnp.float32)
            grad = sums / counts
            moved = 0.9 * mom[:, at, cut].reshape(pair_rows, cut_of) + grad
            stepped = par[:, at, cut].reshape(pair_rows, cut_of) - 0.7 * (grad + 0.9 * moved)
            mom[:, at, cut] = moved.reshape(modules, GROUP, cut_of)
            par[:, at, cut] = stepped.reshape(modules, GROUP, cut_of)
            fresh[:, at, :] = stepped.astype(jnp.bfloat16).reshape(modules, GROUP, cut_of)

        @pl.loop(0, paths)
        def _(path):
            sending[piece, path] = fresh[chosen[path]]

        weight[piece, me] = sending[piece, me]
        for step in ORDER:
            to = shifted(me, step)
            remote(
                sending.at[piece, to], weight.at[piece, me],
                weight_send.at[piece], weight_recv.at[piece], to, sec,
            ).start()

    def turned(src, dst):
        @pl.loop(0, mid // 256)
        def _(block):
            start = pl.multiple_of(block * 256, 256)
            dst[:, pl.ds(start, 256)] = src[pl.ds(start, 256), :].T

    @pl.when(jnp.logical_not(looks))
    def _():
        upper_copy.wait_recv()

    x_rest = acts.at[:, pl.ds(mid, mid)]
    turned(upper, x_rest)

    @pl.when(sec == 0)
    def _():
        for at in range(quarters):
            same(lower.at[spans[at]], forward_send.at[at], forward_recv.at[at]).wait_recv()
        turned(lower, x_first)

    size = x_first.shape[0]
    strip = 128

    def add_squares(ref, first):
        @pl.loop(0, size // strip)
        def _(block):
            at = pl.ds(pl.multiple_of(block * strip, strip), strip)
            held = jnp.zeros((strip, 128), jnp.float32) if first else squares[at, :]
            for start in range(0, ref.shape[1], 128):
                value = ref[at, start:start + 128].astype(jnp.float32)
                held = held + value * value
            squares[at, :] = held

    add_squares(x_rest, True)

    def weights_in(piece):
        same(weight.at[piece, pl.ds(0, others)], weight_send.at[piece], weight_recv.at[piece]).wait_recv()

    per = half_paths // PIECES

    def rest_part(piece):
        total[:, cuts[piece]] = jnp.dot(
            acts[:, mid:], weight[piece, half_paths:].reshape(mid, cut_of),
            preferred_element_type=jnp.float32,
        )

    def first_part(piece, sources):
        lo, hi = sources[0], sources[-1] + 1
        total[:, cuts[piece]] += jnp.dot(
            x_first[:, lo * cut_of:hi * cut_of],
            weight[piece, lo * per:hi * per].reshape((hi - lo) * cut_of, cut_of),
            preferred_element_type=jnp.float32,
        )

    def set_scale():
        @pl.loop(0, size // strip)
        def _(block):
            at = pl.ds(pl.multiple_of(block * strip, strip), strip)
            mean = jnp.sum(squares[at, :], axis=-1, keepdims=True) / model
            squares[at, :] = jnp.broadcast_to(lax.rsqrt(mean + 1e-06), (strip, 128))

    def write(piece):
        @pl.loop(0, size // strip)
        def _(block):
            at = pl.ds(pl.multiple_of(block * strip, strip), strip)
            scale = squares[at, :]
            for start in range(piece * cut_of, (piece + 1) * cut_of, 128):
                cut = pl.ds(start, 128)
                mixed = total[at, cut] * scale
                written = x_first[at, cut].astype(jnp.float32) + jax.nn.silu(mixed)
                acts[at, cut] = written.astype(jnp.bfloat16)

    def hop(piece):
        return remote(
            acts.at[:, cuts[piece]], x_first.at[:, cuts[piece]],
            level_send.at[piece], level_recv.at[piece], me, jnp.minimum(sec + 1, 3),
        )

    everything = list(range(PIECES))

    @pl.when(sec == 0)
    def _():
        add_squares(x_first, False)
        set_scale()
        for piece in everything:
            weights_in(piece)
            rest_part(piece)
            first_part(piece, everything)
            write(piece)
            hop(piece).start()

    @pl.when(sec == 1)
    def _():
        soon = PIECES // 2
        for piece in everything[:soon]:
            weights_in(piece)
            rest_part(piece)
        for source in everything:
            hop(source).wait_recv()
            add_squares(x_first.at[:, cuts[source]], False)
        set_scale()
        for piece in everything:
            if piece >= soon:
                weights_in(piece)
                rest_part(piece)
            first_part(piece, everything)
            write(piece)
            hop(piece).start()

    @pl.when(late)
    def _():
        for piece in everything:
            weights_in(piece)
            rest_part(piece)
        for source in everything[:-1]:
            hop(source).wait_recv()
            add_squares(x_first.at[:, cuts[source]], False)
        for piece in everything:
            first_part(piece, everything[:-1])
        hop(everything[-1]).wait_recv()
        add_squares(x_first.at[:, cuts[-1]], False)
        set_scale()
        for piece in everything:
            first_part(piece, everything[-1:])
            write(piece)

            @pl.when(sec == 2)
            def _():
                hop(piece).start()

    for piece in everything:
        same(pieces.at[pl.ds(0, others), :, cuts[piece]], delta_send.at[piece], delta_recv.at[piece]).wait_send()
        same(weight.at[piece, pl.ds(0, others)], weight_send.at[piece], weight_recv.at[piece]).wait_send()

        @pl.when(sec < 3)
        def _():
            hop(piece).wait_send()

    @pl.when(jnp.logical_not(looks))
    def _():
        loads[0].wait()

    @pl.when(looks)
    def _():
        same(everyone, id_sem.at[0], id_sem.at[1]).wait_send()
        upper_copy.wait_send()
        sent = leaving.at[pl.ds(0, others)]

        @pl.when(holds_upper)
        def _():
            same(sent, upper_send, upper_recv).wait_send()

        @pl.when(sec == 3)
        def _():
            for at in range(quarters):
                passing(at).wait_send()

            @pl.when(jnp.logical_not(holds_upper))
            def _():
                same(sent, lower_send, lower_recv.at[0]).wait_send()


def store(a, b, c, x, y, z, sem):
    copies = [
        pltpu.make_async_copy(src, dst, sem.at[at])
        for at, (src, dst) in enumerate(((a, x), (b, y), (c, z)))
    ]
    for copy in copies:
        copy.start()
    for copy in copies:
        copy.wait()


def local(delta, outer_params, momentum, module_table, token_ids, embedding):
    paths = module_table.shape[1]
    _, modules, rows, wide = outer_params.shape
    vocab, width = embedding.shape
    tok = token_ids.shape[1]
    model = delta.shape[2]
    mid = model // 2
    cut_of = wide // PIECES
    bf16, f32 = jnp.bfloat16, jnp.float32
    anywhere = pl.BlockSpec(memory_space=pl.ANY)
    near = pl.BlockSpec(memory_space=pltpu.VMEM)
    dma = pltpu.SemaphoreType.DMA
    held = pl.pallas_call(
        kernel,
        out_shape=(
            pltpu.VMEM((modules, rows, wide), f32),
            pltpu.VMEM((modules, rows, wide), f32),
            pltpu.VMEM((tok, model), bf16),
        ),
        in_specs=[anywhere, anywhere, anywhere, anywhere, near, pl.BlockSpec(memory_space=pltpu.SMEM)],
        out_specs=(near, near, near),
        scratch_shapes=[
            pltpu.VMEM((paths, rows, wide), bf16),
            pltpu.VMEM((modules, rows, cut_of), bf16),
            pltpu.VMEM((PIECES, paths, rows, cut_of), bf16),
            pltpu.VMEM((PIECES, paths, rows, cut_of), bf16),
            pltpu.VMEM((width, vocab), bf16),
            pltpu.VMEM((vocab, width), f32),
            pltpu.VMEM((8, 128), jnp.int32),
            pltpu.VMEM((paths, 8, 128), jnp.int32),
            pltpu.SMEM((paths, 8, 128), jnp.int32),
            pltpu.VMEM((tok, width), f32),
            pltpu.VMEM((paths, width, tok), bf16),
            pltpu.VMEM((mid, tok), bf16),
            pltpu.VMEM((mid, tok), bf16),
            pltpu.VMEM((tok, mid), bf16),
            pltpu.VMEM((tok, wide), f32),
            pltpu.VMEM((tok, 128), f32),
            dma((8,)), dma((2,)), dma((PIECES,)), dma((PIECES,)), dma((PIECES,)), dma((PIECES,)),
            dma, dma((4,)), dma, dma, dma((4,)), dma((4,)),
            dma((2,)), dma((PIECES,)), dma((PIECES,)),
        ],
        compiler_params=pltpu.CompilerParams(
            collective_id=0, has_side_effects=True, vmem_limit_bytes=46 * 1024 * 1024,
        ),
        name="outer_step",
    )(
        delta.reshape(paths, rows, wide), outer_params[0], momentum[0],
        embedding.T, token_ids, module_table[0, :, 0],
    )
    held = [pltpu.with_memory_space_constraint(value, pltpu.VMEM) for value in held]
    new_params, new_moment, acts = pl.pallas_call(
        store,
        out_shape=tuple(jax.ShapeDtypeStruct(value.shape, value.dtype) for value in held),
        in_specs=[near, near, near],
        out_specs=(anywhere, anywhere, anywhere),
        scratch_shapes=[dma((3,))],
        compiler_params=pltpu.CompilerParams(vmem_limit_bytes=2 * 1024 * 1024),
        name="store",
    )(*held)
    return (new_params[None], new_moment[None], acts[None, None])


def solution(mesh):
    return jax.shard_map(
        local,
        mesh=mesh,
        in_specs=(
            P("section", "path", None, None),
            P("section", None, "path", None),
            P("section", None, "path", None),
            P("section", None, None),
            P("path", None),
            P(None, "path"),
        ),
        out_specs=(
            P("section", None, "path", None),
            P("section", None, "path", None),
            P("section", "path", None, None),
        ),
        check_vma=False,
    )
```

```python
import jax
import jax.numpy as jnp
from jax import lax
from jax.experimental import pallas as pl
from jax.experimental.pallas import tpu as pltpu
from jax.sharding import PartitionSpec as P

MESH = pl.DeviceIdType.MESH
ORDER = [
    (2, 2, 1), (0, 1, 0), (3, 2, 1), (0, 3, 0), (1, 2, 1), (1, 0, 0), (2, 3, 1), (3, 0, 0),
    (2, 1, 1), (0, 0, 1), (2, 2, 0), (1, 1, 0), (2, 1, 0), (3, 3, 0), (2, 3, 0), (1, 3, 0),
    (1, 2, 0), (0, 3, 1), (3, 2, 0), (3, 1, 0), (1, 1, 1), (0, 1, 1), (3, 3, 1), (2, 0, 0),
    (3, 1, 1), (3, 0, 1), (1, 3, 1), (0, 2, 0), (2, 0, 1), (1, 0, 1), (0, 2, 1),
]
PIECES = 4
GATE = 1
GROUP = 16


def shifted(me, step):
    y, z, x = step
    return (
        lax.rem(me // 8 + y, 4) * 8
        + lax.rem(lax.rem(me // 2, 4) + z, 4) * 2
        + lax.rem(lax.rem(me, 2) + x, 2)
    )


def kernel(
    delta, params, moment, table_t, ids, chosen,
    par, mom, acts,
    pieces, fresh, sending, weight,
    columns, table, id_own, id_all, id_scalar, gathered, leaving, relay, lower, upper,
    x_first, total, squares,
    local_sem, id_sem, delta_send, delta_recv, weight_send, weight_recv,
    lookup_send, lookup_recv, cross_send, cross_recv, upper_send, upper_recv, forward_send, forward_recv,
    level_send, level_recv, gate,
):
    me = lax.axis_index("path")
    sec = lax.axis_index("section")
    paths, rows, wide = pieces.shape
    modules = par.shape[0]
    width = table.shape[1]
    model = acts.shape[1]
    mid = model // 2
    cut_of = wide // PIECES
    others = paths - 1
    late = sec >= 2
    looks = late
    half = lax.rem(sec, 2)
    twin = me + 1 - 2 * lax.rem(me, 2)

    def remote(src, dst, send, recv, path, section):
        return pltpu.make_async_remote_copy(
            src_ref=src, dst_ref=dst, send_sem=send, recv_sem=recv,
            device_id=(path, section), device_id_type=MESH,
        )

    def same(ref, send, recv):
        return remote(ref, ref, send, recv, me, sec)

    loads = [
        pltpu.make_async_copy(table_t, columns, local_sem.at[0]),
        pltpu.make_async_copy(params, par, local_sem.at[1]),
        pltpu.make_async_copy(moment, mom, local_sem.at[2]),
    ]
    for load in loads:
        load.start()
    cuts = [pl.ds(piece * cut_of, cut_of) for piece in range(PIECES)]
    own = [
        pltpu.make_async_copy(delta.at[me, :, cuts[piece]], pieces.at[me, :, cuts[piece]], local_sem.at[3 + piece])
        for piece in range(PIECES)
    ]
    for copy in own:
        copy.start()
    tiles = ids.shape[1] // 128
    for tile in range(tiles):
        id_own[tile:tile + 1, :] = ids[:, 128 * tile:128 * (tile + 1)]
    id_own[tiles:, :] = jnp.zeros((8 - tiles, 128), jnp.int32)
    id_all[me] = id_own[...]

    barrier = pltpu.get_barrier_semaphore()
    for step in ORDER:
        pl.semaphore_signal(barrier, inc=1, device_id=(shifted(me, step), sec), device_id_type=MESH)

    @pl.when(sec > 0)
    def _():
        pl.semaphore_signal(barrier, inc=1, device_id=(me, sec - 1), device_id_type=MESH)

    @pl.when(sec < 3)
    def _():
        pl.semaphore_signal(barrier, inc=1, device_id=(me, sec + 1), device_id_type=MESH)

    @pl.when(late)
    def _():
        pl.semaphore_signal(barrier, inc=1, device_id=(twin, 0), device_id_type=MESH)

    @pl.when(sec == 0)
    def _():
        for target in (2, 3):
            pl.semaphore_signal(barrier, inc=1, device_id=(twin, target), device_id_type=MESH)

    pl.semaphore_wait(barrier, others + 2 + jnp.where(half == 0, 1, 0))

    @pl.when(looks)
    def _():
        for step in ORDER:
            remote(id_own, id_all.at[me], id_sem.at[0], id_sem.at[1], shifted(me, step), sec).start()

    def send_delta(piece):
        for step in ORDER:
            to = shifted(me, step)
            remote(
                delta.at[to, :, cuts[piece]], pieces.at[me, :, cuts[piece]],
                delta_send.at[piece], delta_recv.at[piece], to, sec,
            ).start()

    ahead = PIECES // 2

    @pl.when(sec == 1)
    def _():
        pl.semaphore_wait(gate, 1)

    for piece in range(ahead):
        send_delta(piece)

    tokens = gathered.shape[0]
    half_paths = paths // 2
    own_rows = pl.ds(pl.multiple_of(me * width, width), width)
    everyone = id_all.at[pl.ds(0, others)]
    quarters = 4
    holders = paths // quarters
    spans = [pl.ds(at * holders * width, holders * width) for at in range(quarters)]

    @pl.when(looks)
    def _():
        loads[0].wait()

        @pl.loop(0, table.shape[0] // 640)
        def _(block):
            start = pl.multiple_of(block * 640, 640)
            table[pl.ds(start, 640), :] = columns[:, pl.ds(start, 640)].T.astype(jnp.float32)

        same(everyone, id_sem.at[0], id_sem.at[1]).wait_recv()
        ids_in = pltpu.make_async_copy(id_all, id_scalar, local_sem.at[0])
        ids_in.start()
        ids_in.wait()

        @pl.loop(0, paths)
        def _(turn):
            mixed = lax.rem(turn * 13, 32)
            to = shifted(me, (mixed // 8, lax.rem(mixed // 2, 4), lax.rem(mixed, 2)))
            to_twin = to + 1 - 2 * lax.rem(to, 2)

            @pl.loop(0, tokens // 32)
            def _(group):
                line = half * (tokens // 128) + group // 4
                first = lax.rem(group, 4) * 32
                for at in range(32):
                    token = id_scalar[to, line, first + at]
                    gathered[pl.ds(group * 32 + at, 1), :] = table[pl.ds(token, 1), :]

            leaving[to] = gathered[...].T.astype(jnp.bfloat16)

            @pl.when(to_twin != me)
            def _():
                remote(
                    leaving.at[to], relay.at[own_rows],
                    lookup_send, lookup_recv.at[me // holders], to_twin, sec,
                ).start()

        relay[own_rows, :] = leaving[twin]

    def passing(at):
        into = upper if at >= quarters // 2 else lower
        return remote(
            relay.at[spans[at]], into.at[half, spans[at % (quarters // 2)]],
            forward_send.at[at], forward_recv.at[half * quarters + at], twin, 0,
        )

    def crossing(at):
        return remote(
            relay.at[spans[quarters // 2 + at]], upper.at[half, spans[at]],
            cross_send.at[at], cross_recv.at[at], twin, sec,
        )

    def forward():
        for at in (2, 3, 0, 1):
            mine = me // holders == at

            @pl.when(mine)
            def _():
                same(relay.at[pl.ds(0, (holders - 1) * width)], lookup_send, lookup_recv.at[at]).wait_recv()

            @pl.when(jnp.logical_not(mine))
            def _():
                same(relay.at[pl.ds(0, holders * width)], lookup_send, lookup_recv.at[at]).wait_recv()

            passing(at).start()
            if at >= quarters // 2:
                crossing(at - quarters // 2).start()

    for piece in range(ahead, PIECES):
        send_delta(piece)
        if piece == ahead:
            pl.when(looks)(forward)

    def upper_hop(at):
        return remote(upper.at[at], upper.at[at], upper_send.at[at], upper_recv.at[at], me, 1)

    mate = sec + 1 - 2 * half
    trade = remote(upper.at[half], upper.at[half], upper_send.at[0], upper_recv.at[0], me, mate)

    def exchange():
        for at in range(2):
            crossing(at).wait_recv()
        trade.start()

    loads[1].wait()
    loads[2].wait()
    pair_rows, pair_cols = modules * GROUP, paths * GROUP
    col = lax.broadcasted_iota(jnp.int32, (1, pair_cols), 1)
    uses = jnp.zeros((1, pair_cols), jnp.int32)
    for path in range(paths):
        uses = jnp.where(col // GROUP == path, chosen[path], uses)
    row = lax.broadcasted_iota(jnp.int32, (pair_rows, pair_cols), 0)
    cols = lax.broadcasted_iota(jnp.int32, (pair_rows, pair_cols), 1)
    match = (uses == row // GROUP) & (lax.rem(row, GROUP) == lax.rem(cols, GROUP))
    match = match.astype(jnp.float32)
    counts = jnp.maximum(jnp.sum(match, axis=1, keepdims=True), 1.0)
    match = match.astype(jnp.bfloat16)
    for piece in range(PIECES):
        cut = cuts[piece]
        same(pieces.at[pl.ds(0, others), :, cut], delta_send.at[piece], delta_recv.at[piece]).wait_recv()
        own[piece].wait()
        if piece == GATE:
            @pl.when(sec == 0)
            def _():
                pl.semaphore_signal(gate, inc=1, device_id=(me, sec + 1), device_id_type=MESH)

        @pl.loop(0, rows // GROUP)
        def _(group):
            at = pl.ds(pl.multiple_of(group * GROUP, GROUP), GROUP)
            terms = pieces[:, at, cut].reshape(pair_cols, cut_of)
            sums = jnp.dot(match, terms, preferred_element_type=jnp.float32)
            grad = sums / counts
            moved = 0.9 * mom[:, at, cut].reshape(pair_rows, cut_of) + grad
            stepped = par[:, at, cut].reshape(pair_rows, cut_of) - 0.7 * (grad + 0.9 * moved)
            mom[:, at, cut] = moved.reshape(modules, GROUP, cut_of)
            par[:, at, cut] = stepped.reshape(modules, GROUP, cut_of)
            fresh[:, at, :] = stepped.astype(jnp.bfloat16).reshape(modules, GROUP, cut_of)

        @pl.loop(0, paths)
        def _(path):
            sending[piece, path] = fresh[chosen[path]]

        weight[piece, me] = sending[piece, me]
        for step in ORDER:
            to = shifted(me, step)
            remote(
                sending.at[piece, to], weight.at[piece, me],
                weight_send.at[piece], weight_recv.at[piece], to, sec,
            ).start()

    pl.when(late)(exchange)

    def turned(src, dst):
        for side in range(2):
            @pl.loop(0, mid // 256)
            def _(block):
                start = pl.multiple_of(block * 256, 256)
                dst[side * tokens:(side + 1) * tokens, pl.ds(start, 256)] = src[side, pl.ds(start, 256), :].T

    for at in range(2):
        @pl.when(sec == 0)
        def _():
            for part in (2, 3):
                same(upper.at[at, spans[part - 2]], forward_send.at[part], forward_recv.at[at * quarters + part]).wait_recv()

            upper_hop(at).start()

        @pl.when(sec == 1)
        def _():
            upper_hop(at).wait_recv()

    @pl.when(late)
    def _():
        trade.wait_recv()

    x_rest = acts.at[:, pl.ds(mid, mid)]
    turned(upper, x_rest)

    @pl.when(sec == 0)
    def _():
        for at in range(2):
            for part in (0, 1):
                same(lower.at[at, spans[part]], forward_send.at[part], forward_recv.at[at * quarters + part]).wait_recv()
        turned(lower, x_first)

    size = x_first.shape[0]
    strip = 128

    def add_squares(ref, first):
        @pl.loop(0, size // strip)
        def _(block):
            at = pl.ds(pl.multiple_of(block * strip, strip), strip)
            held = jnp.zeros((strip, 128), jnp.float32) if first else squares[at, :]
            for start in range(0, ref.shape[1], 128):
                value = ref[at, start:start + 128].astype(jnp.float32)
                held = held + value * value
            squares[at, :] = held

    add_squares(x_rest, True)

    def weights_in(piece):
        same(weight.at[piece, pl.ds(0, others)], weight_send.at[piece], weight_recv.at[piece]).wait_recv()

    per = half_paths // PIECES

    def rest_part(piece):
        total[:, cuts[piece]] = jnp.dot(
            acts[:, mid:], weight[piece, half_paths:].reshape(mid, cut_of),
            preferred_element_type=jnp.float32,
        )

    def first_part(piece, sources):
        lo, hi = sources[0], sources[-1] + 1
        total[:, cuts[piece]] += jnp.dot(
            x_first[:, lo * cut_of:hi * cut_of],
            weight[piece, lo * per:hi * per].reshape((hi - lo) * cut_of, cut_of),
            preferred_element_type=jnp.float32,
        )

    def set_scale():
        @pl.loop(0, size // strip)
        def _(block):
            at = pl.ds(pl.multiple_of(block * strip, strip), strip)
            mean = jnp.sum(squares[at, :], axis=-1, keepdims=True) / model
            squares[at, :] = jnp.broadcast_to(lax.rsqrt(mean + 1e-06), (strip, 128))

    def write(piece):
        @pl.loop(0, size // strip)
        def _(block):
            at = pl.ds(pl.multiple_of(block * strip, strip), strip)
            scale = squares[at, :]
            for start in range(piece * cut_of, (piece + 1) * cut_of, 128):
                cut = pl.ds(start, 128)
                mixed = total[at, cut] * scale
                written = x_first[at, cut].astype(jnp.float32) + jax.nn.silu(mixed)
                acts[at, cut] = written.astype(jnp.bfloat16)

    def hop(piece):
        return remote(
            acts.at[:, cuts[piece]], x_first.at[:, cuts[piece]],
            level_send.at[piece], level_recv.at[piece], me, jnp.minimum(sec + 1, 3),
        )

    everything = list(range(PIECES))

    @pl.when(sec == 0)
    def _():
        add_squares(x_first, False)
        set_scale()
        for piece in everything:
            weights_in(piece)
            rest_part(piece)
            first_part(piece, everything)
            write(piece)
            hop(piece).start()

    @pl.when(sec == 1)
    def _():
        soon = PIECES // 2
        for piece in everything[:soon]:
            weights_in(piece)
            rest_part(piece)
        for source in everything:
            hop(source).wait_recv()
            add_squares(x_first.at[:, cuts[source]], False)
        set_scale()
        for piece in everything:
            if piece >= soon:
                weights_in(piece)
                rest_part(piece)
            first_part(piece, everything)
            write(piece)
            hop(piece).start()

    @pl.when(late)
    def _():
        for piece in everything:
            weights_in(piece)
            rest_part(piece)
        for source in everything[:-1]:
            hop(source).wait_recv()
            add_squares(x_first.at[:, cuts[source]], False)
        for piece in everything:
            first_part(piece, everything[:-1])
        hop(everything[-1]).wait_recv()
        add_squares(x_first.at[:, cuts[-1]], False)
        set_scale()
        for piece in everything:
            first_part(piece, everything[-1:])
            write(piece)

            @pl.when(sec == 2)
            def _():
                hop(piece).start()

    for piece in everything:
        same(pieces.at[pl.ds(0, others), :, cuts[piece]], delta_send.at[piece], delta_recv.at[piece]).wait_send()
        same(weight.at[piece, pl.ds(0, others)], weight_send.at[piece], weight_recv.at[piece]).wait_send()

        @pl.when(sec < 3)
        def _():
            hop(piece).wait_send()

    @pl.when(jnp.logical_not(looks))
    def _():
        loads[0].wait()

    @pl.when(sec == 0)
    def _():
        for at in range(2):
            upper_hop(at).wait_send()

    @pl.when(looks)
    def _():
        same(everyone, id_sem.at[0], id_sem.at[1]).wait_send()
        same(leaving.at[pl.ds(0, others)], lookup_send, lookup_recv.at[0]).wait_send()
        for at in range(quarters):
            passing(at).wait_send()
        for at in range(2):
            crossing(at).wait_send()
        trade.wait_send()


def store(a, b, c, x, y, z, sem):
    copies = [
        pltpu.make_async_copy(src, dst, sem.at[at])
        for at, (src, dst) in enumerate(((a, x), (b, y), (c, z)))
    ]
    for copy in copies:
        copy.start()
    for copy in copies:
        copy.wait()


def local(delta, outer_params, momentum, module_table, token_ids, embedding):
    paths = module_table.shape[1]
    _, modules, rows, wide = outer_params.shape
    vocab, width = embedding.shape
    tok = token_ids.shape[1]
    model = delta.shape[2]
    mid = model // 2
    cut_of = wide // PIECES
    bf16, f32 = jnp.bfloat16, jnp.float32
    anywhere = pl.BlockSpec(memory_space=pl.ANY)
    near = pl.BlockSpec(memory_space=pltpu.VMEM)
    dma = pltpu.SemaphoreType.DMA
    held = pl.pallas_call(
        kernel,
        out_shape=(
            pltpu.VMEM((modules, rows, wide), f32),
            pltpu.VMEM((modules, rows, wide), f32),
            pltpu.VMEM((tok, model), bf16),
        ),
        in_specs=[anywhere, anywhere, anywhere, anywhere, near, pl.BlockSpec(memory_space=pltpu.SMEM)],
        out_specs=(near, near, near),
        scratch_shapes=[
            pltpu.VMEM((paths, rows, wide), bf16),
            pltpu.VMEM((modules, rows, cut_of), bf16),
            pltpu.VMEM((PIECES, paths, rows, cut_of), bf16),
            pltpu.VMEM((PIECES, paths, rows, cut_of), bf16),
            pltpu.VMEM((width, vocab), bf16),
            pltpu.VMEM((vocab, width), f32),
            pltpu.VMEM((8, 128), jnp.int32),
            pltpu.VMEM((paths, 8, 128), jnp.int32),
            pltpu.SMEM((paths, 8, 128), jnp.int32),
            pltpu.VMEM((tok // 2, width), f32),
            pltpu.VMEM((paths, width, tok // 2), bf16),
            pltpu.VMEM((model, tok // 2), bf16),
            pltpu.VMEM((2, mid, tok // 2), bf16),
            pltpu.VMEM((2, mid, tok // 2), bf16),
            pltpu.VMEM((tok, mid), bf16),
            pltpu.VMEM((tok, wide), f32),
            pltpu.VMEM((tok, 128), f32),
            dma((8,)), dma((2,)), dma((PIECES,)), dma((PIECES,)), dma((PIECES,)), dma((PIECES,)),
            dma, dma((4,)), dma((2,)), dma((2,)), dma((2,)), dma((2,)), dma((4,)), dma((8,)),
            dma((PIECES,)), dma((PIECES,)), pltpu.SemaphoreType.REGULAR,
        ],
        compiler_params=pltpu.CompilerParams(
            collective_id=0, has_side_effects=True, vmem_limit_bytes=46 * 1024 * 1024,
        ),
        name="outer_step",
    )(
        delta.reshape(paths, rows, wide), outer_params[0], momentum[0],
        embedding.T, token_ids, module_table[0, :, 0],
    )
    held = [pltpu.with_memory_space_constraint(value, pltpu.VMEM) for value in held]
    new_params, new_moment, acts = pl.pallas_call(
        store,
        out_shape=tuple(jax.ShapeDtypeStruct(value.shape, value.dtype) for value in held),
        in_specs=[near, near, near],
        out_specs=(anywhere, anywhere, anywhere),
        scratch_shapes=[dma((3,))],
        compiler_params=pltpu.CompilerParams(vmem_limit_bytes=2 * 1024 * 1024),
        name="store",
    )(*held)
    return (new_params[None], new_moment[None], acts[None, None])


def solution(mesh):
    return jax.shard_map(
        local,
        mesh=mesh,
        in_specs=(
            P("section", "path", None, None),
            P("section", None, "path", None),
            P("section", None, "path", None),
            P("section", None, None),
            P("path", None),
            P(None, "path"),
        ),
        out_specs=(
            P("section", None, "path", None),
            P("section", None, "path", None),
            P("section", "path", None, None),
        ),
        check_vma=False,
    )
```

```python
import jax
import jax.numpy as jnp
from jax import lax
from jax.experimental import pallas as pl
from jax.experimental.pallas import tpu as pltpu
from jax.sharding import PartitionSpec as P

MESH = pl.DeviceIdType.MESH
ORDER = [
    (2, 2, 1), (0, 1, 0), (3, 2, 1), (0, 3, 0), (1, 2, 1), (1, 0, 0), (2, 3, 1), (3, 0, 0),
    (2, 1, 1), (0, 0, 1), (2, 2, 0), (1, 1, 0), (2, 1, 0), (3, 3, 0), (2, 3, 0), (1, 3, 0),
    (1, 2, 0), (0, 3, 1), (3, 2, 0), (3, 1, 0), (1, 1, 1), (0, 1, 1), (3, 3, 1), (2, 0, 0),
    (3, 1, 1), (3, 0, 1), (1, 3, 1), (0, 2, 0), (2, 0, 1), (1, 0, 1), (0, 2, 1),
]
PIECES = 4
GROUP = 16


def shifted(me, step):
    y, z, x = step
    return (
        lax.rem(me // 8 + y, 4) * 8
        + lax.rem(lax.rem(me // 2, 4) + z, 4) * 2
        + lax.rem(lax.rem(me, 2) + x, 2)
    )


def kernel(
    delta, params, moment, table_t, ids, chosen,
    par, mom, acts,
    pieces, fresh, sending, weight,
    columns, table, id_own, id_all, id_scalar, gathered, leaving, lower, upper,
    x_first, total, squares,
    local_sem, id_sem, delta_send, delta_recv, weight_send, weight_recv,
    lower_send, lower_recv, upper_send, upper_recv, forward_send, forward_recv,
    core_sem, level_send, level_recv,
):
    me = lax.axis_index("path")
    sec = lax.axis_index("section")
    half = lax.rem(sec, 2)
    mate = sec + 1 - 2 * half
    paths, rows, wide = pieces.shape
    modules = par.shape[0]
    width = table.shape[1]
    model = acts.shape[1]
    mid = model // 2
    cut_of = wide // PIECES
    others = paths - 1
    late = sec >= 2
    looks = half == 1
    holds_upper = me >= paths // 2
    reads = jnp.logical_or(late, holds_upper)
    twin = me + 1 - 2 * lax.rem(me, 2)

    def remote(src, dst, send, recv, path, section):
        return pltpu.make_async_remote_copy(
            src_ref=src, dst_ref=dst, send_sem=send, recv_sem=recv,
            device_id=(path, section), device_id_type=MESH,
        )

    def same(ref, send, recv):
        return remote(ref, ref, send, recv, me, sec)

    loads = [
        pltpu.make_async_copy(table_t, columns, local_sem.at[0]),
        pltpu.make_async_copy(params, par, local_sem.at[1]),
        pltpu.make_async_copy(moment, mom, local_sem.at[2]),
    ]
    for load in loads:
        load.start()
    cuts = [pl.ds(piece * cut_of, cut_of) for piece in range(PIECES)]
    own = [
        pltpu.make_async_copy(delta.at[me, :, cuts[piece]], pieces.at[me, :, cuts[piece]], local_sem.at[3 + piece])
        for piece in range(PIECES)
    ]
    for copy in own:
        copy.start()
    tiles = ids.shape[1] // 128
    for tile in range(tiles):
        id_own[tile:tile + 1, :] = ids[:, 128 * tile:128 * (tile + 1)]
    id_own[tiles:, :] = jnp.zeros((8 - tiles, 128), jnp.int32)
    id_all[me] = id_own[...]

    barrier = pltpu.get_barrier_semaphore()
    for step in ORDER:
        pl.semaphore_signal(barrier, inc=1, device_id=(shifted(me, step), sec), device_id_type=MESH)

    @pl.when(sec > 0)
    def _():
        pl.semaphore_signal(barrier, inc=1, device_id=(me, sec - 1), device_id_type=MESH)

    @pl.when(sec < 3)
    def _():
        pl.semaphore_signal(barrier, inc=1, device_id=(me, sec + 1), device_id_type=MESH)

    @pl.when(jnp.logical_or(sec == 0, sec == 3))
    def _():
        pl.semaphore_signal(barrier, inc=1, device_id=(twin, 3 - sec), device_id_type=MESH)

    pl.semaphore_wait(barrier, others + 2)

    @pl.when(looks)
    def _():
        for step in ORDER:
            remote(id_own, id_all.at[me], id_sem.at[0], id_sem.at[1], shifted(me, step), sec).start()

    def send_delta(piece):
        for step in ORDER:
            to = shifted(me, step)
            remote(
                delta.at[to, :, cuts[piece]], pieces.at[me, :, cuts[piece]],
                delta_send.at[piece], delta_recv.at[piece], to, sec,
            ).start()

    ahead = PIECES - 1
    for piece in range(ahead):
        send_delta(piece)

    tokens = gathered.shape[0]
    half_paths = paths // 2
    slot = lax.rem(me, half_paths)
    own_rows = pl.ds(pl.multiple_of(slot * width, width), width)
    everyone = id_all.at[pl.ds(0, others)]
    quarters = 4
    holders = half_paths // quarters
    spans = [pl.ds(at * holders * width, holders * width) for at in range(quarters)]

    @pl.when(looks)
    def _():
        loads[0].wait()

        @pl.loop(0, table.shape[0] // 640)
        def _(block):
            start = pl.multiple_of(block * 640, 640)
            table[pl.ds(start, 640), :] = columns[:, pl.ds(start, 640)].T.astype(jnp.float32)

        same(everyone, id_sem.at[0], id_sem.at[1]).wait_recv()
        ids_in = pltpu.make_async_copy(id_all, id_scalar, local_sem.at[0])
        ids_in.start()
        ids_in.wait()

        @pl.when(reads)
        def _():
            @pl.loop(0, paths)
            def _(turn):
                mixed = lax.rem(turn * 13, 32)
                to = shifted(me, (mixed // 8, lax.rem(mixed // 2, 4), lax.rem(mixed, 2)))
                to_twin = to + 1 - 2 * lax.rem(to, 2)

                @pl.loop(0, tokens // 64)
                def _(group):
                    line = group // 2
                    first = lax.rem(group, 2) * 64
                    for at in range(64):
                        token = id_scalar[to, line, first + at]
                        gathered[pl.ds(group * 64 + at, 1), :] = table[pl.ds(token, 1), :]

                leaving[to] = gathered[...].T.astype(jnp.bfloat16)

                @pl.when(jnp.logical_and(to_twin != me, jnp.logical_not(holds_upper)))
                def _():
                    remote(
                        leaving.at[to], lower.at[own_rows],
                        lower_send, lower_recv.at[slot // holders], to_twin, sec,
                    ).start()

                @pl.when(jnp.logical_and(to != me, holds_upper))
                def _():
                    remote(leaving.at[to], upper.at[own_rows], upper_send, upper_recv, to, sec).start()

        @pl.when(holds_upper)
        def _():
            upper[own_rows, :] = leaving[me]

        @pl.when(jnp.logical_and(sec == 3, jnp.logical_not(holds_upper)))
        def _():
            lower[own_rows, :] = leaving[twin]

    for piece in range(ahead, PIECES):
        send_delta(piece)

    upper_copy = remote(upper, upper, core_sem.at[0], core_sem.at[1], me, mate)

    def passing(at):
        return remote(
            lower.at[spans[at]], lower.at[spans[at]], forward_send.at[at], forward_recv.at[at], twin, sec - 3
        )

    def forward():
        @pl.when(sec == 3)
        def _():
            for at in range(quarters):
                mine = jnp.logical_and(slot // holders == at, jnp.logical_not(holds_upper))

                @pl.when(mine)
                def _():
                    same(lower.at[pl.ds(0, (holders - 1) * width)], lower_send, lower_recv.at[at]).wait_recv()

                @pl.when(jnp.logical_not(mine))
                def _():
                    same(lower.at[pl.ds(0, holders * width)], lower_send, lower_recv.at[at]).wait_recv()

                passing(at).start()

        @pl.when(holds_upper)
        def _():
            same(upper.at[pl.ds(0, mid - width)], upper_send, upper_recv).wait_recv()

        @pl.when(jnp.logical_not(holds_upper))
        def _():
            same(upper, upper_send, upper_recv).wait_recv()

        upper_copy.start()

    loads[1].wait()
    loads[2].wait()
    pair_rows, pair_cols = modules * GROUP, paths * GROUP
    col = lax.broadcasted_iota(jnp.int32, (1, pair_cols), 1)
    uses = jnp.zeros((1, pair_cols), jnp.int32)
    for path in range(paths):
        uses = jnp.where(col // GROUP == path, chosen[path], uses)
    row = lax.broadcasted_iota(jnp.int32, (pair_rows, pair_cols), 0)
    cols = lax.broadcasted_iota(jnp.int32, (pair_rows, pair_cols), 1)
    match = (uses == row // GROUP) & (lax.rem(row, GROUP) == lax.rem(cols, GROUP))
    match = match.astype(jnp.float32)
    counts = jnp.maximum(jnp.sum(match, axis=1, keepdims=True), 1.0)
    match = match.astype(jnp.bfloat16)
    for piece in range(PIECES):
        if piece == PIECES // 2:
            pl.when(looks)(forward)
        cut = cuts[piece]
        same(pieces.at[pl.ds(0, others), :, cut], delta_send.at[piece], delta_recv.at[piece]).wait_recv()
        own[piece].wait()

        @pl.loop(0, rows // GROUP)
        def _(group):
            at = pl.ds(pl.multiple_of(group * GROUP, GROUP), GROUP)
            terms = pieces[:, at, cut].reshape(pair_cols, cut_of)
            sums = jnp.dot(match, terms, preferred_element_type=jnp.float32)
            grad = sums / counts
            moved = 0.9 * mom[:, at, cut].reshape(pair_rows, cut_of) + grad
            stepped = par[:, at, cut].reshape(pair_rows, cut_of) - 0.7 * (grad + 0.9 * moved)
            mom[:, at, cut] = moved.reshape(modules, GROUP, cut_of)
            par[:, at, cut] = stepped.reshape(modules, GROUP, cut_of)
            fresh[:, at, :] = stepped.astype(jnp.bfloat16).reshape(modules, GROUP, cut_of)

        @pl.loop(0, paths)
        def _(path):
            sending[piece, path] = fresh[chosen[path]]

        weight[piece, me] = sending[piece, me]
        for step in ORDER:
            to = shifted(me, step)
            remote(
                sending.at[piece, to], weight.at[piece, me],
                weight_send.at[piece], weight_recv.at[piece], to, sec,
            ).start()

    def turned(src, dst):
        @pl.loop(0, mid // 256)
        def _(block):
            start = pl.multiple_of(block * 256, 256)
            dst[:, pl.ds(start, 256)] = src[pl.ds(start, 256), :].T

    @pl.when(jnp.logical_not(looks))
    def _():
        upper_copy.wait_recv()

    x_rest = acts.at[:, pl.ds(mid, mid)]
    turned(upper, x_rest)

    @pl.when(sec == 0)
    def _():
        for at in range(quarters):
            same(lower.at[spans[at]], forward_send.at[at], forward_recv.at[at]).wait_recv()
        turned(lower, x_first)

    size = x_first.shape[0]
    strip = 128

    def add_squares(ref, first):
        @pl.loop(0, size // strip)
        def _(block):
            at = pl.ds(pl.multiple_of(block * strip, strip), strip)
            held = jnp.zeros((strip, 128), jnp.float32) if first else squares[at, :]
            for start in range(0, ref.shape[1], 128):
                value = ref[at, start:start + 128].astype(jnp.float32)
                held = held + value * value
            squares[at, :] = held

    add_squares(x_rest, True)

    def weights_in(piece):
        same(weight.at[piece, pl.ds(0, others)], weight_send.at[piece], weight_recv.at[piece]).wait_recv()

    per = half_paths // PIECES

    def rest_part(piece):
        total[:, cuts[piece]] = jnp.dot(
            acts[:, mid:], weight[piece, half_paths:].reshape(mid, cut_of),
            preferred_element_type=jnp.float32,
        )

    def first_part(piece, sources):
        lo, hi = sources[0], sources[-1] + 1
        total[:, cuts[piece]] += jnp.dot(
            x_first[:, lo * cut_of:hi * cut_of],
            weight[piece, lo * per:hi * per].reshape((hi - lo) * cut_of, cut_of),
            preferred_element_type=jnp.float32,
        )

    def set_scale():
        @pl.loop(0, size // strip)
        def _(block):
            at = pl.ds(pl.multiple_of(block * strip, strip), strip)
            mean = jnp.sum(squares[at, :], axis=-1, keepdims=True) / model
            squares[at, :] = jnp.broadcast_to(lax.rsqrt(mean + 1e-06), (strip, 128))

    def write(piece):
        @pl.loop(0, size // strip)
        def _(block):
            at = pl.ds(pl.multiple_of(block * strip, strip), strip)
            scale = squares[at, :]
            for start in range(piece * cut_of, (piece + 1) * cut_of, 128):
                cut = pl.ds(start, 128)
                mixed = total[at, cut] * scale
                written = x_first[at, cut].astype(jnp.float32) + jax.nn.silu(mixed)
                acts[at, cut] = written.astype(jnp.bfloat16)

    def hop(piece):
        return remote(
            acts.at[:, cuts[piece]], x_first.at[:, cuts[piece]],
            level_send.at[piece], level_recv.at[piece], me, jnp.minimum(sec + 1, 3),
        )

    everything = list(range(PIECES))

    @pl.when(sec == 0)
    def _():
        add_squares(x_first, False)
        set_scale()
        for piece in everything:
            weights_in(piece)
            rest_part(piece)
            first_part(piece, everything)
            write(piece)
            hop(piece).start()

    @pl.when(sec == 1)
    def _():
        soon = PIECES // 2
        for piece in everything[:soon]:
            weights_in(piece)
            rest_part(piece)
        for source in everything:
            hop(source).wait_recv()
            add_squares(x_first.at[:, cuts[source]], False)
        set_scale()
        for piece in everything:
            if piece >= soon:
                weights_in(piece)
                rest_part(piece)
            first_part(piece, everything)
            write(piece)
            hop(piece).start()

    @pl.when(late)
    def _():
        for piece in everything:
            weights_in(piece)
            rest_part(piece)
        for source in everything[:-1]:
            hop(source).wait_recv()
            add_squares(x_first.at[:, cuts[source]], False)
        for piece in everything:
            first_part(piece, everything[:-1])
        hop(everything[-1]).wait_recv()
        add_squares(x_first.at[:, cuts[-1]], False)
        set_scale()
        for piece in everything:
            first_part(piece, everything[-1:])
            write(piece)

            @pl.when(sec == 2)
            def _():
                hop(piece).start()

    for piece in everything:
        same(pieces.at[pl.ds(0, others), :, cuts[piece]], delta_send.at[piece], delta_recv.at[piece]).wait_send()
        same(weight.at[piece, pl.ds(0, others)], weight_send.at[piece], weight_recv.at[piece]).wait_send()

        @pl.when(sec < 3)
        def _():
            hop(piece).wait_send()

    @pl.when(jnp.logical_not(looks))
    def _():
        loads[0].wait()

    @pl.when(looks)
    def _():
        same(everyone, id_sem.at[0], id_sem.at[1]).wait_send()
        upper_copy.wait_send()
        sent = leaving.at[pl.ds(0, others)]

        @pl.when(holds_upper)
        def _():
            same(sent, upper_send, upper_recv).wait_send()

        @pl.when(sec == 3)
        def _():
            for at in range(quarters):
                passing(at).wait_send()

            @pl.when(jnp.logical_not(holds_upper))
            def _():
                same(sent, lower_send, lower_recv.at[0]).wait_send()


def store(a, b, c, x, y, z, sem):
    copies = [
        pltpu.make_async_copy(src, dst, sem.at[at])
        for at, (src, dst) in enumerate(((a, x), (b, y), (c, z)))
    ]
    for copy in copies:
        copy.start()
    for copy in copies:
        copy.wait()


def local(delta, outer_params, momentum, module_table, token_ids, embedding):
    paths = module_table.shape[1]
    _, modules, rows, wide = outer_params.shape
    vocab, width = embedding.shape
    tok = token_ids.shape[1]
    model = delta.shape[2]
    mid = model // 2
    cut_of = wide // PIECES
    bf16, f32 = jnp.bfloat16, jnp.float32
    anywhere = pl.BlockSpec(memory_space=pl.ANY)
    near = pl.BlockSpec(memory_space=pltpu.VMEM)
    dma = pltpu.SemaphoreType.DMA
    held = pl.pallas_call(
        kernel,
        out_shape=(
            pltpu.VMEM((modules, rows, wide), f32),
            pltpu.VMEM((modules, rows, wide), f32),
            pltpu.VMEM((tok, model), bf16),
        ),
        in_specs=[anywhere, anywhere, anywhere, anywhere, near, pl.BlockSpec(memory_space=pltpu.SMEM)],
        out_specs=(near, near, near),
        scratch_shapes=[
            pltpu.VMEM((paths, rows, wide), bf16),
            pltpu.VMEM((modules, rows, cut_of), bf16),
            pltpu.VMEM((PIECES, paths, rows, cut_of), bf16),
            pltpu.VMEM((PIECES, paths, rows, cut_of), bf16),
            pltpu.VMEM((width, vocab), bf16),
            pltpu.VMEM((vocab, width), f32),
            pltpu.VMEM((8, 128), jnp.int32),
            pltpu.VMEM((paths, 8, 128), jnp.int32),
            pltpu.SMEM((paths, 8, 128), jnp.int32),
            pltpu.VMEM((tok, width), f32),
            pltpu.VMEM((paths, width, tok), bf16),
            pltpu.VMEM((mid, tok), bf16),
            pltpu.VMEM((mid, tok), bf16),
            pltpu.VMEM((tok, mid), bf16),
            pltpu.VMEM((tok, wide), f32),
            pltpu.VMEM((tok, 128), f32),
            dma((8,)), dma((2,)), dma((PIECES,)), dma((PIECES,)), dma((PIECES,)), dma((PIECES,)),
            dma, dma((4,)), dma, dma, dma((4,)), dma((4,)),
            dma((2,)), dma((PIECES,)), dma((PIECES,)),
        ],
        compiler_params=pltpu.CompilerParams(
            collective_id=0, has_side_effects=True, vmem_limit_bytes=46 * 1024 * 1024,
        ),
        name="outer_step",
    )(
        delta.reshape(paths, rows, wide), outer_params[0], momentum[0],
        embedding.T, token_ids, module_table[0, :, 0],
    )
    held = [pltpu.with_memory_space_constraint(value, pltpu.VMEM) for value in held]
    new_params, new_moment, acts = pl.pallas_call(
        store,
        out_shape=tuple(jax.ShapeDtypeStruct(value.shape, value.dtype) for value in held),
        in_specs=[near, near, near],
        out_specs=(anywhere, anywhere, anywhere),
        scratch_shapes=[dma((3,))],
        compiler_params=pltpu.CompilerParams(vmem_limit_bytes=2 * 1024 * 1024),
        name="store",
    )(*held)
    return (new_params[None], new_moment[None], acts[None, None])


def solution(mesh):
    return jax.shard_map(
        local,
        mesh=mesh,
        in_specs=(
            P("section", "path", None, None),
            P("section", None, "path", None),
            P("section", None, "path", None),
            P("section", None, None),
            P("path", None),
            P(None, "path"),
        ),
        out_specs=(
            P("section", None, "path", None),
            P("section", None, "path", None),
            P("section", "path", None, None),
        ),
        check_vma=False,
    )
```
